512 devices in a mesh: inst: 64 (over x_lo, z, core), tp: 8 (over y, x_hi).
Axes of the slice: x: 4 (x_hi: 2, x_lo: 2; x = x_hi * 2 + x_lo), y: 4, z: 16, core: 2. Of those that a mesh axis runs over, the one named last changes fastest.
Arguments:
- queries: bfloat16 [2, 4, 768, 8192], P(None, None, 'inst', 'tp'), may hold values from -125 to 125
- cache_keys: bfloat16 [2, 768, 128, 1024], P(None, 'inst', None, 'tp'), may hold values from -4.5 to 4.5
- cache_values: bfloat16 [2, 768, 128, 1024], P(None, 'inst', None, 'tp'), may hold values from -6 to 6
- new_keys: bfloat16 [2, 4, 768, 1024], P(None, None, 'inst', 'tp'), may hold values from -8 to 8
- new_values: bfloat16 [2, 4, 768, 1024], P(None, None, 'inst', 'tp'), may hold values from -6 to 6
- kv_pool: bfloat16 [5120, 2, 2, 16, 1024], P('inst', None, None, None, 'tp'), may hold values from -6 to 6
- mig_lengths: int32 [64], replicated, may hold values from 256 to 1024, as said below
- mig_source: int32 [64], replicated, may hold values from 0 to 63, as said below
- mig_target: int32 [64], replicated, may hold values from 0 to 63, as said below
- block_lists: int32 [64, 64], replicated, may hold values from 0 to 79, as said below
- owner_map: int32 [64, 64], replicated, may hold values from 0 to 127
- check_key: bfloat16 [2, 2, 1024, 128], P(None, None, 'tp'), may hold values from -0.5 to 0.5
Outputs:
- attention: bfloat16 [2, 4, 768, 8192], P(None, None, 'inst', 'tp')
- arrived: bfloat16 [4096, 2, 2, 16, 1024], P('inst', None, None, None, 'tp')
- checksums: float32 [128, 128], P('inst')
The draws below stay inside these ranges and needn't reach their ends.
Inputs may be any that keep to these rules, and one draw needn't show every extreme that they name: `mig_lengths`: some request has exactly 1024 tokens and some exactly 256. `mig_source`: each instance drains exactly one request. `mig_target`: each instance receives exactly one request, never its own. `block_lists`: the slots of one row are distinct.
All inputs are finite; a program needn't handle non-finite values.
Results may differ from the reference program's by a relative error of at most 0.015.
Values may be sent and summed in bfloat16 or wider, within the bound.
No kernel may reach another device: no remote copies, remote signals or barrier semaphores. Data moves between devices by JAX's collectives and lax.ppermute only.
A program may use at most 64 MiB of HBM per device.

```python
import math
import jax
import jax.numpy as jnp
from jax import lax

QH = 64
KVH = 8
HD = 128
CSUM = 128
LAYERS = 2
STEPS = 4
BLOCK = 16
MAXBLK = 64
REQ_DEC = 12
CTX = 128
QW = 8192
KW = 1024
REQS = 768
MIGS = 64
POOL = 80
MAXLEN = 1024
CHECKS = 128
N_INST = 64


def pair_order(key):
    first = jax.random.permutation(jax.random.fold_in(key, 11), MIGS).astype(jnp.int32)
    cycle = jax.random.permutation(jax.random.fold_in(key, 12), MIGS).astype(jnp.int32)
    following = jnp.zeros((MIGS,), jnp.int32).at[cycle].set(jnp.roll(cycle, -1))
    return (first, following[first])


def key_field(key):
    base = jax.random.normal(jax.random.fold_in(key, 21), (LAYERS, REQS, CTX, KW), jnp.float32)
    return jnp.clip(base, -4.0, 4.0)


def draw_mig_source(key, part):
    return pair_order(key)[0]


def draw_mig_target(key, part):
    return pair_order(key)[1]


def draw_mig_lengths(key, part):
    key = jax.random.fold_in(key, 3)
    lengths = jax.random.randint(key, (MIGS,), MAXLEN // 4, MAXLEN + 1).astype(jnp.int32)
    chosen = jax.random.randint(jax.random.fold_in(key, 4), (), 0, MIGS)
    order = jnp.arange(MIGS, dtype=jnp.int32)
    lengths = jnp.where(order == chosen, MAXLEN, lengths)
    lengths = jnp.where(order == (chosen + 1) % MIGS, MAXLEN // 4, lengths)
    return lengths.astype(jnp.int32)


def draw_block_lists(key, part):
    key = jax.random.fold_in(key, 5)
    keys = jax.random.split(key, MIGS)
    rows = jax.vmap(lambda single: jax.random.permutation(single, POOL)[:MAXBLK])(keys)
    return rows.astype(jnp.int32)


def draw_cache_keys(key, part):
    base = key_field(key)
    return base.astype(jnp.bfloat16)


def draw_queries(key, part):
    key = jax.random.fold_in(key, 7)
    fresh = jnp.clip(jax.random.normal(key, (LAYERS, STEPS, REQS, QW), jnp.float32), -4.0, 4.0)
    return fresh.astype(jnp.bfloat16)


def place_ends(array, stream_key, least, largest):
    spot = [jax.random.randint(jax.random.fold_in(stream_key, axis), (), 0, length) for axis, length in enumerate(array.shape)]
    main_axis = array.shape.index(max(array.shape))
    next_to = spot[:main_axis] + [(spot[main_axis] + 1) % array.shape[main_axis]] + spot[main_axis + 1:]
    return array.at[tuple(spot)].set(least).at[tuple(next_to)].set(largest)


def steps_of(stream_key, extent, shards, low, largest):
    factor_of, own = 1.0, jax.random.fold_in(stream_key, 6)
    for dim, parts in shards:
        steps = jnp.exp(jax.random.uniform(jax.random.fold_in(own, dim), (parts,), jnp.float32, low / len(shards), largest / len(shards)))
        factor_of = factor_of * jnp.repeat(steps, extent[dim] // parts).reshape([-1 if axis == dim else 1 for axis in range(len(extent))])
    return factor_of


def scatter_about(key, extent, scale, bound, cuts=(), kind=jnp.bfloat16):
    array = scale * jax.random.normal(key, extent, jnp.float32)
    if cuts:
        array = array * steps_of(key, extent, cuts, -0.22, 0.18)
    return jnp.clip(array, -bound, bound).astype(kind)


def setup_inputs(seed: int = 0) -> dict:
    arg_keys = jax.random.split(jax.random.key(seed), 13)
    return {
        "queries": draw_queries(jax.random.fold_in(arg_keys[12], 71), 0),
        "cache_keys": draw_cache_keys(jax.random.fold_in(arg_keys[12], 71), 0),
        "cache_values": scatter_about(arg_keys[2], (LAYERS, REQS, CTX, KW), 1.0, 6.0, ((1, 64), (3, 8))),
        "new_keys": scatter_about(arg_keys[3], (LAYERS, STEPS, REQS, KW), 2.0, 8.0, ((2, 64), (3, 8))),
        "new_values": scatter_about(arg_keys[4], (LAYERS, STEPS, REQS, KW), 1.0, 6.0, ((2, 64), (3, 8))),
        "kv_pool": scatter_about(arg_keys[5], (MIGS * POOL, LAYERS, 2, BLOCK, KW), 1.0, 6.0, ((0, 64), (4, 8))),
        "mig_lengths": draw_mig_lengths(jax.random.fold_in(arg_keys[12], 71), 0),
        "mig_source": draw_mig_source(jax.random.fold_in(arg_keys[12], 71), 0),
        "mig_target": draw_mig_target(jax.random.fold_in(arg_keys[12], 71), 0),
        "block_lists": draw_block_lists(jax.random.fold_in(arg_keys[12], 71), 0),
        "owner_map": place_ends(jax.random.randint(arg_keys[10], (MIGS, MAXBLK), 0, CHECKS), jax.random.fold_in(arg_keys[10], 1), 0, CHECKS - 1).astype(jnp.int32),
        "check_key": scatter_about(arg_keys[11], (LAYERS, 2, KW, CSUM), HD ** -0.5, 0.5, ((2, 8),)),
    }


def attend_group(inputs):
    query, keyed, valued, fresh_keys, fresh_values = inputs
    group = QH // KVH
    rows = query.shape[2]
    query = query.astype(jnp.float32).reshape(LAYERS, STEPS, rows, KVH, group, HD)
    keyed = keyed.astype(jnp.float32).reshape(LAYERS, rows, CTX, KVH, HD)
    valued = valued.astype(jnp.float32).reshape(LAYERS, rows, CTX, KVH, HD)
    fresh_keys = fresh_keys.astype(jnp.float32).reshape(LAYERS, STEPS, rows, KVH, HD)
    fresh_values = fresh_values.astype(jnp.float32).reshape(LAYERS, STEPS, rows, KVH, HD)
    layer_outs = []
    for layer in range(LAYERS):
        step_outs = []
        for step in range(STEPS):
            all_keys = jnp.concatenate([keyed[layer], jnp.moveaxis(fresh_keys[layer, :step + 1], 0, 1)], axis=1)
            all_values = jnp.concatenate([valued[layer], jnp.moveaxis(fresh_values[layer, :step + 1], 0, 1)], axis=1)
            scores = jnp.einsum('rkgd,rckd->rkgc', query[layer, step], all_keys) / math.sqrt(HD)
            highest = lax.optimization_barrier(jnp.max(scores, axis=-1, keepdims=True))
            expd = jnp.exp(scores - highest)
            weights = (expd / lax.optimization_barrier(jnp.sum(expd, axis=-1, keepdims=True))).astype(jnp.bfloat16)
            weights = lax.optimization_barrier(weights).astype(jnp.float32)
            mixed = jnp.einsum('rkgc,rckd->rkgd', weights, all_values)
            step_outs.append(mixed.astype(jnp.bfloat16).reshape(rows, QW))
        layer_outs.append(jnp.stack(step_outs))
    return jnp.stack(layer_outs)

def reference(queries, cache_keys, cache_values, new_keys, new_values, kv_pool, mig_lengths, mig_source, mig_target, block_lists, owner_map, check_key):
    grouped = (queries.reshape(LAYERS, STEPS, N_INST, REQ_DEC, QW).transpose(2, 0, 1, 3, 4), cache_keys.reshape(LAYERS, N_INST, REQ_DEC, CTX, KW).transpose(1, 0, 2, 3, 4), cache_values.reshape(LAYERS, N_INST, REQ_DEC, CTX, KW).transpose(1, 0, 2, 3, 4), new_keys.reshape(LAYERS, STEPS, N_INST, REQ_DEC, KW).transpose(2, 0, 1, 3, 4), new_values.reshape(LAYERS, STEPS, N_INST, REQ_DEC, KW).transpose(2, 0, 1, 3, 4))
    attended = lax.map(attend_group, grouped)
    attention = attended.transpose(1, 2, 0, 3, 4).reshape(LAYERS, STEPS, REQS, QW)
    rows = (mig_source[:, None] * POOL + block_lists).astype(jnp.int32)
    taken = kv_pool[rows]
    position = jnp.arange(MAXBLK, dtype=jnp.int32)[:, None] * BLOCK + jnp.arange(BLOCK, dtype=jnp.int32)[None, :]
    live = position[None, :, :] < mig_lengths[:, None, None]
    taken = jnp.where(live[:, :, None, None, :, None], taken, jnp.zeros((), kv_pool.dtype))
    arrived = jnp.zeros_like(taken).at[mig_target].set(taken)
    arrived = arrived.reshape(MIGS * MAXBLK, LAYERS, 2, BLOCK, KW)
    projection = check_key.astype(jnp.float32).reshape(LAYERS, 2, KVH, HD, CSUM)

    def digest_one(request_blocks):
        grid = request_blocks.astype(jnp.float32).reshape(MAXBLK, LAYERS, 2, BLOCK, KVH, HD)
        projected = jnp.einsum('blktgd,lkgde->blktge', grid, projection, precision=lax.Precision.HIGHEST)
        return lax.optimization_barrier(jnp.sum(jnp.tanh(projected), axis=(1, 2, 3, 4))) / 16.0
    digest = lax.map(digest_one, taken)
    checksums = jnp.zeros((CHECKS, CSUM), jnp.float32).at[owner_map.reshape(-1)].add(digest.reshape(-1, CSUM))
    return (attention, arrived, checksums)
```

```python
import math

import jax
import jax.numpy as jnp
from jax import lax
from jax.sharding import PartitionSpec as P

HD = 128
SLOTS = 2


def decode_attention(queries, cache_keys, cache_values, new_keys, new_values):
    layers, steps, requests, qwidth = queries.shape
    context = cache_keys.shape[2]
    kwidth = cache_keys.shape[3]
    heads_local = kwidth // HD
    grouping = qwidth // kwidth
    query = queries.reshape(layers, steps, requests, heads_local, grouping, HD)
    keyed = cache_keys.reshape(layers, requests, context, heads_local, HD)
    valued = cache_values.reshape(layers, requests, context, heads_local, HD)
    fresh_keys = new_keys.reshape(layers, steps, requests, heads_local, HD)
    fresh_values = new_values.reshape(layers, steps, requests, heads_local, HD)
    factor = 1.0 / math.sqrt(HD)
    old_scores = (
        jnp.einsum("lsrkgd,lrckd->lsrkgc", query, keyed, preferred_element_type=jnp.float32)
        * factor
    )
    new_scores = (
        jnp.einsum("lsrkgd,ltrkd->lsrkgt", query, fresh_keys, preferred_element_type=jnp.float32)
        * factor
    )
    order = jnp.arange(steps)
    visible = (order[None, :] <= order[:, None])[None, :, None, None, None, :]
    new_scores = jnp.where(visible, new_scores, -1e30)
    highest = jnp.maximum(
        jnp.max(old_scores, axis=-1, keepdims=True), jnp.max(new_scores, axis=-1, keepdims=True)
    )
    old_exp = jnp.exp(old_scores - highest)
    new_exp = jnp.where(visible, jnp.exp(new_scores - highest), 0.0)
    denominator = jnp.sum(old_exp, axis=-1, keepdims=True) + jnp.sum(
        new_exp, axis=-1, keepdims=True
    )
    old_weights = (old_exp / denominator).astype(jnp.bfloat16)
    new_weights = (new_exp / denominator).astype(jnp.bfloat16)
    mixed = jnp.einsum(
        "lsrkgc,lrckd->lsrkgd", old_weights, valued, preferred_element_type=jnp.float32
    )
    mixed = mixed + jnp.einsum(
        "lsrkgt,ltrkd->lsrkgd", new_weights, fresh_values, preferred_element_type=jnp.float32
    )
    return mixed.astype(jnp.bfloat16).reshape(layers, steps, requests, qwidth)


def local(
    queries,
    cache_keys,
    cache_values,
    new_keys,
    new_values,
    kv_pool,
    mig_lengths,
    mig_source,
    mig_target,
    block_lists,
    owner_map,
    check_key,
):
    attention = decode_attention(queries, cache_keys, cache_values, new_keys, new_values)
    members = lax.axis_size("inst")
    heads = lax.axis_size("tp")
    place = lax.axis_index("inst")
    request_ids = jnp.arange(mig_source.shape[0], dtype=jnp.int32)
    own_request = jnp.sum(jnp.where(mig_source == place, request_ids, 0))
    length = mig_lengths[own_request]
    slot_row = block_lists[own_request]
    blocks = kv_pool[slot_row]
    depth, layers, pair, span, width = blocks.shape
    position = jnp.arange(depth)[:, None] * span + jnp.arange(span)[None, :]
    blocks = jnp.where(
        (position < length)[:, None, None, :, None], blocks, jnp.zeros((), blocks.dtype)
    )
    sectioned = lax.all_to_all(blocks, "inst", split_axis=0, concat_axis=0, tiled=True)

    projected = jnp.einsum("blktd,lkde->blkte", blocks, check_key, preferred_element_type=jnp.float32)
    digest = jnp.sum(jnp.tanh(projected), axis=(1, 2, 3)) / 16.0
    owners = owner_map[own_request]
    table_rows = SLOTS * members
    one_hot = (owners[None, :] == jnp.arange(table_rows)[:, None]).astype(jnp.float32)
    table = jnp.dot(one_hot, digest, precision=lax.Precision.HIGHEST, preferred_element_type=jnp.float32)
    reach = 1
    while reach < heads:
        table = table + lax.ppermute(table, "tp", [(i, i ^ reach) for i in range(heads)])
        reach *= 2
    terms = table.astype(jnp.bfloat16).reshape(members, 1, SLOTS, table.shape[-1])

    source_of = jnp.sum(
        jnp.where(mig_target[None, :] == request_ids[:, None], mig_source[None, :], 0), axis=1
    )
    onward = sectioned[source_of].reshape(members, -1, SLOTS, width)
    landed = lax.all_to_all(
        jnp.concatenate([onward, terms], axis=1), "inst", split_axis=0, concat_axis=0, tiled=True
    )
    arrived = landed[:, :-1].reshape(blocks.shape)
    checksums = jnp.sum(landed[:, -1].astype(jnp.float32), axis=0)
    return (attention, arrived, checksums)


def solution(mesh):
    placed = (
        P(None, None, "inst", "tp"),
        P(None, "inst", None, "tp"),
        P(None, "inst", None, "tp"),
        P(None, None, "inst", "tp"),
        P(None, None, "inst", "tp"),
        P("inst", None, None, None, "tp"),
        P(),
        P(),
        P(),
        P(),
        P(),
        P(None, None, "tp", None),
    )
    return jax.shard_map(
        local,
        mesh=mesh,
        in_specs=placed,
        out_specs=(P(None, None, "inst", "tp"), P("inst", None, None, None, "tp"), P("inst", None)),
        check_vma=False,
    )
```

```python
import math

import jax
import jax.numpy as jnp
from jax import lax
from jax.sharding import PartitionSpec as P

HD = 128
SLOTS = 2


def decode_attention(queries, cache_keys, cache_values, new_keys, new_values):
    layers, steps, requests, qwidth = queries.shape
    context = cache_keys.shape[2]
    kwidth = cache_keys.shape[3]
    heads_local = kwidth // HD
    grouping = qwidth // kwidth
    query = queries.reshape(layers, steps, requests, heads_local, grouping, HD)
    keyed = cache_keys.reshape(layers, requests, context, heads_local, HD)
    valued = cache_values.reshape(layers, requests, context, heads_local, HD)
    fresh_keys = new_keys.reshape(layers, steps, requests, heads_local, HD)
    fresh_values = new_values.reshape(layers, steps, requests, heads_local, HD)
    factor = 1.0 / math.sqrt(HD)
    old_scores = (
        jnp.einsum("lsrkgd,lrckd->lsrkgc", query, keyed, preferred_element_type=jnp.float32)
        * factor
    )
    new_scores = (
        jnp.einsum("lsrkgd,ltrkd->lsrkgt", query, fresh_keys, preferred_element_type=jnp.float32)
        * factor
    )
    order = jnp.arange(steps)
    visible = (order[None, :] <= order[:, None])[None, :, None, None, None, :]
    new_scores = jnp.where(visible, new_scores, -1e30)
    highest = jnp.maximum(
        jnp.max(old_scores, axis=-1, keepdims=True), jnp.max(new_scores, axis=-1, keepdims=True)
    )
    old_exp = jnp.exp(old_scores - highest)
    new_exp = jnp.where(visible, jnp.exp(new_scores - highest), 0.0)
    denominator = jnp.sum(old_exp, axis=-1, keepdims=True) + jnp.sum(
        new_exp, axis=-1, keepdims=True
    )
    old_weights = (old_exp / denominator).astype(jnp.bfloat16)
    new_weights = (new_exp / denominator).astype(jnp.bfloat16)
    mixed = jnp.einsum(
        "lsrkgc,lrckd->lsrkgd", old_weights, valued, preferred_element_type=jnp.float32
    )
    mixed = mixed + jnp.einsum(
        "lsrkgt,ltrkd->lsrkgd", new_weights, fresh_values, preferred_element_type=jnp.float32
    )
    return mixed.astype(jnp.bfloat16).reshape(layers, steps, requests, qwidth)


def local(
    queries,
    cache_keys,
    cache_values,
    new_keys,
    new_values,
    kv_pool,
    mig_lengths,
    mig_source,
    mig_target,
    block_lists,
    owner_map,
    check_key,
):
    attention = decode_attention(queries, cache_keys, cache_values, new_keys, new_values)
    members = lax.axis_size("inst")
    heads = lax.axis_size("tp")
    place = lax.axis_index("inst")
    request_ids = jnp.arange(mig_source.shape[0], dtype=jnp.int32)
    own_request = jnp.sum(jnp.where(mig_source == place, request_ids, 0))
    length = mig_lengths[own_request]
    slot_row = block_lists[own_request]
    blocks = kv_pool[slot_row]
    depth, span = blocks.shape[0], blocks.shape[3]
    position = jnp.arange(depth)[:, None] * span + jnp.arange(span)[None, :]
    blocks = jnp.where(
        (position < length)[:, None, None, :, None], blocks, jnp.zeros((), blocks.dtype)
    )
    sectioned = lax.all_to_all(blocks, "inst", split_axis=0, concat_axis=0, tiled=True)

    projected = jnp.einsum("blktd,lkde->blkte", blocks, check_key, preferred_element_type=jnp.float32)
    digest = jnp.sum(jnp.tanh(projected), axis=(1, 2, 3)) / 16.0
    owners = owner_map[own_request]
    table_rows = SLOTS * members
    one_hot = (owners[None, :] == jnp.arange(table_rows)[:, None]).astype(jnp.float32)
    table = jnp.dot(one_hot, digest, precision=lax.Precision.HIGHEST, preferred_element_type=jnp.float32)
    part = table
    reach = members // 2
    while reach:
        half = part.shape[0] // 2
        upper = (place // reach) % 2 == 1
        low, high = part[:half], part[half:]
        away = jnp.where(upper, low, high)
        part = jnp.where(upper, high, low) + lax.ppermute(
            away, "inst", [(i, i ^ reach) for i in range(members)]
        )
        reach //= 2
    reach = 1
    while reach < heads:
        part = part + lax.ppermute(part, "tp", [(i, i ^ reach) for i in range(heads)])
        reach *= 2
    checksums = part

    source_of = jnp.sum(
        jnp.where(mig_target[None, :] == request_ids[:, None], mig_source[None, :], 0), axis=1
    )
    arrived = lax.all_to_all(
        sectioned[source_of], "inst", split_axis=0, concat_axis=0, tiled=True
    )
    return (attention, arrived, checksums)


def solution(mesh):
    placed = (
        P(None, None, "inst", "tp"),
        P(None, "inst", None, "tp"),
        P(None, "inst", None, "tp"),
        P(None, None, "inst", "tp"),
        P(None, None, "inst", "tp"),
        P("inst", None, None, None, "tp"),
        P(),
        P(),
        P(),
        P(),
        P(),
        P(None, None, "tp", None),
    )
    return jax.shard_map(
        local,
        mesh=mesh,
        in_specs=placed,
        out_specs=(P(None, None, "inst", "tp"), P("inst", None, None, None, "tp"), P("inst", None)),
        check_vma=False,
    )
```

```python
import math

import jax
import jax.numpy as jnp
from jax import lax
from jax.experimental import pallas as pl
from jax.experimental.pallas import tpu as pltpu
from jax.sharding import PartitionSpec as P

HD = 128
SLOTS = 2


def decode_attention(queries, cache_keys, cache_values, new_keys, new_values):
    layers, steps, requests, qwidth = queries.shape
    context = cache_keys.shape[2]
    kwidth = cache_keys.shape[3]
    heads_local = kwidth // HD
    grouping = qwidth // kwidth
    query = queries.reshape(layers, steps, requests, heads_local, grouping, HD)
    keyed = cache_keys.reshape(layers, requests, context, heads_local, HD)
    valued = cache_values.reshape(layers, requests, context, heads_local, HD)
    fresh_keys = new_keys.reshape(layers, steps, requests, heads_local, HD)
    fresh_values = new_values.reshape(layers, steps, requests, heads_local, HD)
    factor = 1.0 / math.sqrt(HD)
    old_scores = (
        jnp.einsum("lsrkgd,lrckd->lsrkgc", query, keyed, preferred_element_type=jnp.float32)
        * factor
    )
    new_scores = (
        jnp.einsum("lsrkgd,ltrkd->lsrkgt", query, fresh_keys, preferred_element_type=jnp.float32)
        * factor
    )
    order = jnp.arange(steps)
    visible = (order[None, :] <= order[:, None])[None, :, None, None, None, :]
    new_scores = jnp.where(visible, new_scores, -1e30)
    highest = jnp.maximum(
        jnp.max(old_scores, axis=-1, keepdims=True), jnp.max(new_scores, axis=-1, keepdims=True)
    )
    old_exp = jnp.exp(old_scores - highest)
    new_exp = jnp.where(visible, jnp.exp(new_scores - highest), 0.0)
    denominator = jnp.sum(old_exp, axis=-1, keepdims=True) + jnp.sum(
        new_exp, axis=-1, keepdims=True
    )
    old_weights = (old_exp / denominator).astype(jnp.bfloat16)
    new_weights = (new_exp / denominator).astype(jnp.bfloat16)
    mixed = jnp.einsum(
        "lsrkgc,lrckd->lsrkgd", old_weights, valued, preferred_element_type=jnp.float32
    )
    mixed = mixed + jnp.einsum(
        "lsrkgt,ltrkd->lsrkgd", new_weights, fresh_values, preferred_element_type=jnp.float32
    )
    return mixed.astype(jnp.bfloat16).reshape(layers, steps, requests, qwidth)


def take_kernel(source_ref, length_ref, list_ref, pool_ref, own_ref, out_ref):
    place = lax.axis_index("inst")
    step = pl.program_id(0)
    rows, span = out_ref.shape[0], out_ref.shape[3]

    @pl.when(step == 0)
    def _():
        def find(i, found):
            return jnp.where(source_ref[i] == place, i, found)

        own_ref[0] = lax.fori_loop(0, source_ref.shape[0], find, jnp.int32(0), unroll=8)

    own = own_ref[0]
    length = length_ref[own]

    def take(b, carry):
        first = (step * rows + b) * span
        slot = list_ref[own, step * rows + b]
        block = pool_ref[slot]
        token = first + lax.broadcasted_iota(jnp.int32, block.shape, 2)
        out_ref[b] = jnp.where(token < length, block.astype(jnp.float32), 0.0).astype(block.dtype)
        return carry

    lax.fori_loop(0, rows, take, 0, unroll=4)


def take_blocks(mig_source, mig_lengths, block_lists, kv_pool):
    depth = block_lists.shape[1]
    rows = depth // 4
    smem = pl.BlockSpec(memory_space=pltpu.SMEM)
    return pl.pallas_call(
        take_kernel,
        grid=(depth // rows,),
        in_specs=[smem, smem, smem, pl.BlockSpec(memory_space=pltpu.VMEM)],
        out_specs=[
            pl.BlockSpec(memory_space=pltpu.SMEM),
            pl.BlockSpec((rows,) + kv_pool.shape[1:], lambda i: (i, 0, 0, 0, 0)),
        ],
        out_shape=[
            jax.ShapeDtypeStruct((1,), jnp.int32),
            jax.ShapeDtypeStruct((depth,) + kv_pool.shape[1:], kv_pool.dtype),
        ],
        compiler_params=pltpu.CompilerParams(vmem_limit_bytes=16 * 1024 * 1024),
    )(mig_source, mig_lengths, block_lists, kv_pool)


def relay_kernel(source_ref, target_ref, held_ref, terms_ref, out_ref, sems):
    pieces = held_ref.shape[1]
    whole = out_ref.at[:, pl.ds(0, pieces)]
    rest = pltpu.make_async_copy(terms_ref, out_ref.at[:, pl.ds(pieces, 1)], sems.at[1])
    rest.start()

    def send(r, carry):
        pltpu.make_async_copy(
            held_ref.at[source_ref[r]],
            out_ref.at[target_ref[r], pl.ds(0, pieces)],
            sems.at[0],
        ).start()
        return carry

    lax.fori_loop(0, source_ref.shape[0], send, 0, unroll=8)
    pltpu.make_async_copy(held_ref, whole, sems.at[0]).wait()
    rest.wait()


def order_by_target(mig_source, mig_target, held, terms):
    smem = pl.BlockSpec(memory_space=pltpu.SMEM)
    anywhere = pl.BlockSpec(memory_space=pl.ANY)
    return pl.pallas_call(
        relay_kernel,
        in_specs=[smem, smem, anywhere, anywhere],
        out_specs=anywhere,
        out_shape=jax.ShapeDtypeStruct(
            (held.shape[0], held.shape[1] + 1) + held.shape[2:], held.dtype
        ),
        scratch_shapes=[pltpu.SemaphoreType.DMA((2,))],
    )(mig_source, mig_target, held, terms)


def split_kernel(landed_ref, arrived_ref, sums_ref, terms, sems):
    pieces = arrived_ref.shape[1]
    blocks = pltpu.make_async_copy(landed_ref.at[:, pl.ds(0, pieces)], arrived_ref, sems.at[0])
    blocks.start()
    rest = pltpu.make_async_copy(landed_ref.at[:, pl.ds(pieces, 1)], terms, sems.at[1])
    rest.start()
    rest.wait()
    sums_ref[...] = jnp.sum(terms[:, 0].astype(jnp.float32), axis=0)
    blocks.wait()


def split_landed(landed):
    members, pieces, slots, width = landed.shape
    anywhere = pl.BlockSpec(memory_space=pl.ANY)
    return pl.pallas_call(
        split_kernel,
        in_specs=[anywhere],
        out_specs=[anywhere, pl.BlockSpec(memory_space=pltpu.VMEM)],
        out_shape=[
            jax.ShapeDtypeStruct((members, pieces - 1, slots, width), landed.dtype),
            jax.ShapeDtypeStruct((slots, width), jnp.float32),
        ],
        scratch_shapes=[
            pltpu.VMEM((members, 1, slots, width), landed.dtype),
            pltpu.SemaphoreType.DMA((2,)),
        ],
    )(landed)


def local(
    queries,
    cache_keys,
    cache_values,
    new_keys,
    new_values,
    kv_pool,
    mig_lengths,
    mig_source,
    mig_target,
    block_lists,
    owner_map,
    check_key,
):
    attention = decode_attention(queries, cache_keys, cache_values, new_keys, new_values)
    members = lax.axis_size("inst")
    heads = lax.axis_size("tp")
    own_request, blocks = take_blocks(mig_source, mig_lengths, block_lists, kv_pool)
    own_request = own_request[0]
    width = blocks.shape[-1]
    sectioned = lax.all_to_all(blocks, "inst", split_axis=0, concat_axis=0, tiled=True)

    projected = jnp.einsum("blktd,lkde->blkte", blocks, check_key, preferred_element_type=jnp.float32)
    digest = jnp.sum(jnp.tanh(projected), axis=(1, 2, 3)) / 16.0
    owners = owner_map[own_request]
    table_rows = SLOTS * members
    one_hot = (owners[None, :] == jnp.arange(table_rows)[:, None]).astype(jnp.float32)
    table = jnp.dot(one_hot, digest, precision=lax.Precision.HIGHEST, preferred_element_type=jnp.float32)
    reach = 1
    while reach < heads:
        table = table + lax.ppermute(table, "tp", [(i, i ^ reach) for i in range(heads)])
        reach *= 2
    terms = table.astype(jnp.bfloat16).reshape(members, 1, SLOTS, table.shape[-1])

    onward = order_by_target(
        mig_source, mig_target, sectioned.reshape(members, -1, SLOTS, width), terms
    )
    landed = lax.all_to_all(onward, "inst", split_axis=0, concat_axis=0, tiled=True)
    arrived, checksums = split_landed(landed)
    arrived = arrived.reshape(blocks.shape)
    return (attention, arrived, checksums)


def solution(mesh):
    placed = (
        P(None, None, "inst", "tp"),
        P(None, "inst", None, "tp"),
        P(None, "inst", None, "tp"),
        P(None, None, "inst", "tp"),
        P(None, None, "inst", "tp"),
        P("inst", None, None, None, "tp"),
        P(),
        P(),
        P(),
        P(),
        P(),
        P(None, None, "tp", None),
    )
    return jax.shard_map(
        local,
        mesh=mesh,
        in_specs=placed,
        out_specs=(P(None, None, "inst", "tp"), P("inst", None, None, None, "tp"), P("inst", None)),
        check_vma=False,
    )
```

```python
import math

import jax
import jax.numpy as jnp
from jax import lax
from jax.experimental import pallas as pl
from jax.experimental.pallas import tpu as pltpu
from jax.sharding import PartitionSpec as P

HD = 128
SLOTS = 2


def decode_attention(queries, cache_keys, cache_values, new_keys, new_values):
    layers, steps, requests, qwidth = queries.shape
    context = cache_keys.shape[2]
    kwidth = cache_keys.shape[3]
    heads_local = kwidth // HD
    grouping = qwidth // kwidth
    query = queries.reshape(layers, steps, requests, heads_local, grouping, HD)
    keyed = cache_keys.reshape(layers, requests, context, heads_local, HD)
    valued = cache_values.reshape(layers, requests, context, heads_local, HD)
    fresh_keys = new_keys.reshape(layers, steps, requests, heads_local, HD)
    fresh_values = new_values.reshape(layers, steps, requests, heads_local, HD)
    factor = 1.0 / math.sqrt(HD)
    old_scores = (
        jnp.einsum("lsrkgd,lrckd->lsrkgc", query, keyed, preferred_element_type=jnp.float32)
        * factor
    )
    new_scores = (
        jnp.einsum("lsrkgd,ltrkd->lsrkgt", query, fresh_keys, preferred_element_type=jnp.float32)
        * factor
    )
    order = jnp.arange(steps)
    visible = (order[None, :] <= order[:, None])[None, :, None, None, None, :]
    new_scores = jnp.where(visible, new_scores, -1e30)
    highest = jnp.maximum(
        jnp.max(old_scores, axis=-1, keepdims=True), jnp.max(new_scores, axis=-1, keepdims=True)
    )
    old_exp = jnp.exp(old_scores - highest)
    new_exp = jnp.where(visible, jnp.exp(new_scores - highest), 0.0)
    denominator = jnp.sum(old_exp, axis=-1, keepdims=True) + jnp.sum(
        new_exp, axis=-1, keepdims=True
    )
    old_weights = (old_exp / denominator).astype(jnp.bfloat16)
    new_weights = (new_exp / denominator).astype(jnp.bfloat16)
    mixed = jnp.einsum(
        "lsrkgc,lrckd->lsrkgd", old_weights, valued, preferred_element_type=jnp.float32
    )
    mixed = mixed + jnp.einsum(
        "lsrkgt,ltrkd->lsrkgd", new_weights, fresh_values, preferred_element_type=jnp.float32
    )
    return mixed.astype(jnp.bfloat16).reshape(layers, steps, requests, qwidth)


def take_kernel(
    source_hbm, length_hbm, list_hbm, pool_hbm, own_ref, out_hbm, source, lengths, lists, pool, stage, sems
):
    fetches = [
        pltpu.make_async_copy(*pair, sems.at[n])
        for n, pair in enumerate(
            [(source_hbm, source), (length_hbm, lengths), (list_hbm, lists), (pool_hbm, pool)]
        )
    ]
    for fetch in fetches:
        fetch.start()
    place = lax.axis_index("inst")
    depth, span = stage.shape[0], stage.shape[3]
    rows = depth // 4
    fetches[0].wait()
    own = jnp.int32(0)
    for i in range(source.shape[0]):
        own = jnp.where(source[i] == place, jnp.int32(i), own)
    own_ref[0] = own
    for fetch in fetches[1:]:
        fetch.wait()
    length = lengths[own]

    def clear(b, carry):
        block = stage[b]
        token = b * span + lax.broadcasted_iota(jnp.int32, block.shape, 2)
        stage[b] = jnp.where(token < length, block.astype(jnp.float32), 0.0).astype(block.dtype)
        return carry

    writes = []
    for n in range(depth // rows):
        for b in range(n * rows, (n + 1) * rows):
            stage[b] = pool[lists[own, b]]
        lax.fori_loop(jnp.maximum(length // span, n * rows), (n + 1) * rows, clear, 0)
        part = pl.ds(n * rows, rows)
        writes.append(pltpu.make_async_copy(stage.at[part], out_hbm.at[part], sems.at[4 + n]))
        writes[-1].start()
    for write in writes:
        write.wait()


def take_blocks(mig_source, mig_lengths, block_lists, kv_pool):
    depth = block_lists.shape[1]
    return pl.pallas_call(
        take_kernel,
        in_specs=[pl.BlockSpec(memory_space=pltpu.HBM)] * 4,
        out_specs=[
            pl.BlockSpec(memory_space=pltpu.SMEM),
            pl.BlockSpec(memory_space=pltpu.HBM),
        ],
        out_shape=[
            jax.ShapeDtypeStruct((1,), jnp.int32),
            jax.ShapeDtypeStruct((depth,) + kv_pool.shape[1:], kv_pool.dtype),
        ],
        scratch_shapes=[
            pltpu.SMEM(mig_source.shape, jnp.int32),
            pltpu.SMEM(mig_lengths.shape, jnp.int32),
            pltpu.SMEM(block_lists.shape, jnp.int32),
            pltpu.VMEM(kv_pool.shape, kv_pool.dtype),
            pltpu.VMEM((depth,) + kv_pool.shape[1:], kv_pool.dtype),
            pltpu.SemaphoreType.DMA((8,)),
        ],
        compiler_params=pltpu.CompilerParams(vmem_limit_bytes=60 * 1024 * 1024),
    )(mig_source, mig_lengths, block_lists, kv_pool)


def local(
    queries,
    cache_keys,
    cache_values,
    new_keys,
    new_values,
    kv_pool,
    mig_lengths,
    mig_source,
    mig_target,
    block_lists,
    owner_map,
    check_key,
):
    attention = decode_attention(queries, cache_keys, cache_values, new_keys, new_values)
    members = lax.axis_size("inst")
    heads = lax.axis_size("tp")
    request_ids = jnp.arange(mig_source.shape[0], dtype=jnp.int32)
    own_request, blocks = take_blocks(mig_source, mig_lengths, block_lists, kv_pool)
    own_request = own_request[0]
    width = blocks.shape[-1]
    sectioned = lax.all_to_all(blocks, "inst", split_axis=0, concat_axis=0, tiled=True)

    projected = jnp.einsum("blktd,lkde->blkte", blocks, check_key, preferred_element_type=jnp.float32)
    digest = jnp.sum(jnp.tanh(projected), axis=(1, 2, 3)) / 16.0
    owners = owner_map[own_request]
    table_rows = SLOTS * members
    one_hot = (owners[None, :] == jnp.arange(table_rows)[:, None]).astype(jnp.float32)
    table = jnp.dot(one_hot, digest, precision=lax.Precision.HIGHEST, preferred_element_type=jnp.float32)
    reach = 1
    while reach < heads:
        table = table + lax.ppermute(table, "tp", [(i, i ^ reach) for i in range(heads)])
        reach *= 2
    terms = table.astype(jnp.bfloat16).reshape(members, 1, SLOTS, table.shape[-1])

    source_of = jnp.sum(
        jnp.where(mig_target[None, :] == request_ids[:, None], mig_source[None, :], 0), axis=1
    )
    onward = sectioned[source_of].reshape(members, -1, SLOTS, width)
    landed = lax.all_to_all(
        jnp.concatenate([onward, terms], axis=1), "inst", split_axis=0, concat_axis=0, tiled=True
    )
    arrived = landed[:, :-1].reshape(blocks.shape)
    checksums = jnp.sum(landed[:, -1].astype(jnp.float32), axis=0)
    return (attention, arrived, checksums)


def solution(mesh):
    placed = (
        P(None, None, "inst", "tp"),
        P(None, "inst", None, "tp"),
        P(None, "inst", None, "tp"),
        P(None, None, "inst", "tp"),
        P(None, None, "inst", "tp"),
        P("inst", None, None, None, "tp"),
        P(),
        P(),
        P(),
        P(),
        P(),
        P(None, None, "tp", None),
    )
    return jax.shard_map(
        local,
        mesh=mesh,
        in_specs=placed,
        out_specs=(P(None, None, "inst", "tp"), P("inst", None, None, None, "tp"), P("inst", None)),
        check_vma=False,
    )
```

```python
import math

import jax
import jax.numpy as jnp
from jax import lax
from jax.experimental import pallas as pl
from jax.experimental.pallas import tpu as pltpu
from jax.sharding import PartitionSpec as P

HD = 128
SLOTS = 2


def decode_attention(queries, cache_keys, cache_values, new_keys, new_values):
    layers, steps, requests, qwidth = queries.shape
    context = cache_keys.shape[2]
    kwidth = cache_keys.shape[3]
    heads_local = kwidth // HD
    grouping = qwidth // kwidth
    query = queries.reshape(layers, steps, requests, heads_local, grouping, HD)
    keyed = cache_keys.reshape(layers, requests, context, heads_local, HD)
    valued = cache_values.reshape(layers, requests, context, heads_local, HD)
    fresh_keys = new_keys.reshape(layers, steps, requests, heads_local, HD)
    fresh_values = new_values.reshape(layers, steps, requests, heads_local, HD)
    factor = 1.0 / math.sqrt(HD)
    old_scores = (
        jnp.einsum("lsrkgd,lrckd->lsrkgc", query, keyed, preferred_element_type=jnp.float32)
        * factor
    )
    new_scores = (
        jnp.einsum("lsrkgd,ltrkd->lsrkgt", query, fresh_keys, preferred_element_type=jnp.float32)
        * factor
    )
    order = jnp.arange(steps)
    visible = (order[None, :] <= order[:, None])[None, :, None, None, None, :]
    new_scores = jnp.where(visible, new_scores, -1e30)
    highest = jnp.maximum(
        jnp.max(old_scores, axis=-1, keepdims=True), jnp.max(new_scores, axis=-1, keepdims=True)
    )
    old_exp = jnp.exp(old_scores - highest)
    new_exp = jnp.where(visible, jnp.exp(new_scores - highest), 0.0)
    denominator = jnp.sum(old_exp, axis=-1, keepdims=True) + jnp.sum(
        new_exp, axis=-1, keepdims=True
    )
    old_weights = (old_exp / denominator).astype(jnp.bfloat16)
    new_weights = (new_exp / denominator).astype(jnp.bfloat16)
    mixed = jnp.einsum(
        "lsrkgc,lrckd->lsrkgd", old_weights, valued, preferred_element_type=jnp.float32
    )
    mixed = mixed + jnp.einsum(
        "lsrkgt,ltrkd->lsrkgd", new_weights, fresh_values, preferred_element_type=jnp.float32
    )
    return mixed.astype(jnp.bfloat16).reshape(layers, steps, requests, qwidth)


def take_kernel(
    source_hbm, length_hbm, list_hbm, pool_hbm, own_ref, out_hbm, source, lengths, lists, pool, stage, sems
):
    fetches = [
        pltpu.make_async_copy(*pair, sems.at[n])
        for n, pair in enumerate(
            [(source_hbm, source), (length_hbm, lengths), (list_hbm, lists), (pool_hbm, pool)]
        )
    ]
    for fetch in fetches:
        fetch.start()
    place = lax.axis_index("inst")
    depth, span = stage.shape[0], stage.shape[3]
    rows = depth // 4
    fetches[0].wait()
    own = jnp.int32(0)
    for i in range(source.shape[0]):
        own = jnp.where(source[i] == place, jnp.int32(i), own)
    own_ref[0] = own
    for fetch in fetches[1:]:
        fetch.wait()
    length = lengths[own]

    def clear(b, carry):
        block = stage[b]
        token = b * span + lax.broadcasted_iota(jnp.int32, block.shape, 2)
        stage[b] = jnp.where(token < length, block.astype(jnp.float32), 0.0).astype(block.dtype)
        return carry

    writes = []
    for n in range(depth // rows):
        for b in range(n * rows, (n + 1) * rows):
            stage[b] = pool[lists[own, b]]
        lax.fori_loop(jnp.maximum(length // span, n * rows), (n + 1) * rows, clear, 0)
        part = pl.ds(n * rows, rows)
        writes.append(pltpu.make_async_copy(stage.at[part], out_hbm.at[part], sems.at[4 + n]))
        writes[-1].start()
    for write in writes:
        write.wait()


def take_blocks(mig_source, mig_lengths, block_lists, kv_pool):
    depth = block_lists.shape[1]
    return pl.pallas_call(
        take_kernel,
        in_specs=[pl.BlockSpec(memory_space=pltpu.HBM)] * 4,
        out_specs=[
            pl.BlockSpec(memory_space=pltpu.SMEM),
            pl.BlockSpec(memory_space=pltpu.HBM),
        ],
        out_shape=[
            jax.ShapeDtypeStruct((1,), jnp.int32),
            jax.ShapeDtypeStruct((depth,) + kv_pool.shape[1:], kv_pool.dtype),
        ],
        scratch_shapes=[
            pltpu.SMEM(mig_source.shape, jnp.int32),
            pltpu.SMEM(mig_lengths.shape, jnp.int32),
            pltpu.SMEM(block_lists.shape, jnp.int32),
            pltpu.VMEM(kv_pool.shape, kv_pool.dtype),
            pltpu.VMEM((depth,) + kv_pool.shape[1:], kv_pool.dtype),
            pltpu.SemaphoreType.DMA((8,)),
        ],
        compiler_params=pltpu.CompilerParams(vmem_limit_bytes=60 * 1024 * 1024),
    )(mig_source, mig_lengths, block_lists, kv_pool)


def relay_kernel(source_ref, target_ref, held_ref, terms_ref, out_ref, source_of):
    depth = held_ref.shape[0]
    rows = held_ref.shape[1]
    group = 8

    terms = terms_ref[...]
    for r in range(depth):
        source_of[target_ref[r]] = source_ref[r]
    for first in range(0, depth, group):
        pieces = []
        for t in range(first, first + group):
            pieces.append(held_ref[source_of[t]])
            pieces.append(terms[t * SLOTS : (t + 1) * SLOTS])
        size = (rows + SLOTS) * group
        whole = jnp.concatenate(pieces, axis=0)
        out_ref[pl.ds(first * (rows + SLOTS), size)] = whole.astype(out_ref.dtype)


def order_by_target(mig_source, mig_target, held, terms):
    smem = pl.BlockSpec(memory_space=pltpu.SMEM)
    vmem = pl.BlockSpec(memory_space=pltpu.VMEM)
    return pl.pallas_call(
        relay_kernel,
        in_specs=[smem, smem, vmem, vmem],
        out_specs=vmem,
        out_shape=jax.ShapeDtypeStruct(
            (held.shape[0] * (held.shape[1] + SLOTS), held.shape[2]), held.dtype
        ),
        scratch_shapes=[pltpu.SMEM(mig_target.shape, jnp.int32)],
        compiler_params=pltpu.CompilerParams(vmem_limit_bytes=16 * 1024 * 1024),
    )(mig_source, mig_target, held, terms)


def split_kernel(landed_ref, arrived_hbm, sums_ref, stage, sems):
    depth, rows = stage.shape[:2]
    group = 8
    total = jnp.zeros(sums_ref.shape, jnp.float32)
    writes = []
    for first in range(0, depth, group):
        size = (rows + SLOTS) * group
        whole = landed_ref[pl.ds(first * (rows + SLOTS), size)]
        for j in range(group):
            base = j * (rows + SLOTS)
            stage[first + j] = whole[base : base + rows].astype(stage.dtype)
            total = total + whole[base + rows : base + rows + SLOTS].astype(jnp.float32)
        part = pl.ds(first, group)
        writes.append(pltpu.make_async_copy(stage.at[part], arrived_hbm.at[part], sems.at[first // group]))
        writes[-1].start()
    sums_ref[...] = total
    for write in writes:
        write.wait()


def split_landed(landed, depth):
    rows = landed.shape[0] // depth - SLOTS
    width = landed.shape[1]
    vmem = pl.BlockSpec(memory_space=pltpu.VMEM)
    return pl.pallas_call(
        split_kernel,
        in_specs=[vmem],
        out_specs=[pl.BlockSpec(memory_space=pl.ANY), vmem],
        out_shape=[
            jax.ShapeDtypeStruct((depth, rows, width), landed.dtype),
            jax.ShapeDtypeStruct((SLOTS, width), jnp.float32),
        ],
        scratch_shapes=[
            pltpu.VMEM((depth, rows, width), landed.dtype),
            pltpu.SemaphoreType.DMA((depth // 8,)),
        ],
        compiler_params=pltpu.CompilerParams(vmem_limit_bytes=16 * 1024 * 1024),
    )(landed)


def local(
    queries,
    cache_keys,
    cache_values,
    new_keys,
    new_values,
    kv_pool,
    mig_lengths,
    mig_source,
    mig_target,
    block_lists,
    owner_map,
    check_key,
):
    attention = decode_attention(queries, cache_keys, cache_values, new_keys, new_values)
    members = lax.axis_size("inst")
    heads = lax.axis_size("tp")
    own_request, blocks = take_blocks(mig_source, mig_lengths, block_lists, kv_pool)
    own_request = own_request[0]
    width = blocks.shape[-1]
    sectioned = lax.all_to_all(blocks, "inst", split_axis=0, concat_axis=0, tiled=True)

    projected = jnp.einsum("blktd,lkde->blkte", blocks, check_key, preferred_element_type=jnp.float32)
    digest = jnp.sum(jnp.tanh(projected), axis=(1, 2, 3)) / 16.0
    owners = owner_map[own_request]
    table_rows = SLOTS * members
    one_hot = (owners[None, :] == jnp.arange(table_rows)[:, None]).astype(jnp.float32)
    table = jnp.dot(one_hot, digest, precision=lax.Precision.HIGHEST, preferred_element_type=jnp.float32)
    reach = 1
    while reach < heads:
        table = table + lax.ppermute(table, "tp", [(i, i ^ reach) for i in range(heads)])
        reach *= 2
    terms = table.astype(jnp.bfloat16)

    onward = order_by_target(mig_source, mig_target, sectioned.reshape(members, -1, width), terms)
    landed = lax.all_to_all(
        onward.reshape(members, -1, SLOTS, width), "inst", split_axis=0, concat_axis=0, tiled=True
    )
    arrived, checksums = split_landed(landed.reshape(onward.shape), members)
    arrived = arrived.reshape(blocks.shape)
    return (attention, arrived, checksums)


def solution(mesh):
    placed = (
        P(None, None, "inst", "tp"),
        P(None, "inst", None, "tp"),
        P(None, "inst", None, "tp"),
        P(None, None, "inst", "tp"),
        P(None, None, "inst", "tp"),
        P("inst", None, None, None, "tp"),
        P(),
        P(),
        P(),
        P(),
        P(),
        P(None, None, "tp", None),
    )
    return jax.shard_map(
        local,
        mesh=mesh,
        in_specs=placed,
        out_specs=(P(None, None, "inst", "tp"), P("inst", None, None, None, "tp"), P("inst", None)),
        check_vma=False,
    )
```

```python
import math

import jax
import jax.numpy as jnp
from jax import lax
from jax.experimental import pallas as pl
from jax.experimental.pallas import tpu as pltpu
from jax.sharding import PartitionSpec as P

HD = 128
SLOTS = 2


def decode_attention(queries, cache_keys, cache_values, new_keys, new_values):
    layers, steps, requests, qwidth = queries.shape
    context = cache_keys.shape[2]
    kwidth = cache_keys.shape[3]
    heads_local = kwidth // HD
    grouping = qwidth // kwidth
    query = queries.reshape(layers, steps, requests, heads_local, grouping, HD)
    keyed = cache_keys.reshape(layers, requests, context, heads_local, HD)
    valued = cache_values.reshape(layers, requests, context, heads_local, HD)
    fresh_keys = new_keys.reshape(layers, steps, requests, heads_local, HD)
    fresh_values = new_values.reshape(layers, steps, requests, heads_local, HD)
    factor = 1.0 / math.sqrt(HD)
    old_scores = (
        jnp.einsum("lsrkgd,lrckd->lsrkgc", query, keyed, preferred_element_type=jnp.float32)
        * factor
    )
    new_scores = (
        jnp.einsum("lsrkgd,ltrkd->lsrkgt", query, fresh_keys, preferred_element_type=jnp.float32)
        * factor
    )
    order = jnp.arange(steps)
    visible = (order[None, :] <= order[:, None])[None, :, None, None, None, :]
    new_scores = jnp.where(visible, new_scores, -1e30)
    highest = jnp.maximum(
        jnp.max(old_scores, axis=-1, keepdims=True), jnp.max(new_scores, axis=-1, keepdims=True)
    )
    old_exp = jnp.exp(old_scores - highest)
    new_exp = jnp.where(visible, jnp.exp(new_scores - highest), 0.0)
    denominator = jnp.sum(old_exp, axis=-1, keepdims=True) + jnp.sum(
        new_exp, axis=-1, keepdims=True
    )
    old_weights = (old_exp / denominator).astype(jnp.bfloat16)
    new_weights = (new_exp / denominator).astype(jnp.bfloat16)
    mixed = jnp.einsum(
        "lsrkgc,lrckd->lsrkgd", old_weights, valued, preferred_element_type=jnp.float32
    )
    mixed = mixed + jnp.einsum(
        "lsrkgt,ltrkd->lsrkgd", new_weights, fresh_values, preferred_element_type=jnp.float32
    )
    return mixed.astype(jnp.bfloat16).reshape(layers, steps, requests, qwidth)


def take_kernel(
    source_hbm, length_hbm, list_hbm, pool_hbm, own_ref, out_hbm, source, lengths, lists, pool, stage, sems
):
    fetches = [
        pltpu.make_async_copy(*pair, sems.at[n])
        for n, pair in enumerate(
            [(source_hbm, source), (length_hbm, lengths), (list_hbm, lists), (pool_hbm, pool)]
        )
    ]
    for fetch in fetches:
        fetch.start()
    place = lax.axis_index("inst")
    depth, span = stage.shape[0], stage.shape[3]
    rows = depth // 4
    fetches[0].wait()
    own = jnp.int32(0)
    for i in range(source.shape[0]):
        own = jnp.where(source[i] == place, jnp.int32(i), own)
    own_ref[0] = own
    for fetch in fetches[1:]:
        fetch.wait()
    length = lengths[own]

    def clear(b, carry):
        block = stage[b]
        token = b * span + lax.broadcasted_iota(jnp.int32, block.shape, 2)
        stage[b] = jnp.where(token < length, block.astype(jnp.float32), 0.0).astype(block.dtype)
        return carry

    writes = []
    for n in range(depth // rows):
        for b in range(n * rows, (n + 1) * rows):
            stage[b] = pool[lists[own, b]]
        lax.fori_loop(jnp.maximum(length // span, n * rows), (n + 1) * rows, clear, 0)
        part = pl.ds(n * rows, rows)
        writes.append(pltpu.make_async_copy(stage.at[part], out_hbm.at[part], sems.at[4 + n]))
        writes[-1].start()
    for write in writes:
        write.wait()


def take_blocks(mig_source, mig_lengths, block_lists, kv_pool):
    depth = block_lists.shape[1]
    return pl.pallas_call(
        take_kernel,
        in_specs=[pl.BlockSpec(memory_space=pltpu.HBM)] * 4,
        out_specs=[
            pl.BlockSpec(memory_space=pltpu.SMEM),
            pl.BlockSpec(memory_space=pltpu.HBM),
        ],
        out_shape=[
            jax.ShapeDtypeStruct((1,), jnp.int32),
            jax.ShapeDtypeStruct((depth,) + kv_pool.shape[1:], kv_pool.dtype),
        ],
        scratch_shapes=[
            pltpu.SMEM(mig_source.shape, jnp.int32),
            pltpu.SMEM(mig_lengths.shape, jnp.int32),
            pltpu.SMEM(block_lists.shape, jnp.int32),
            pltpu.VMEM(kv_pool.shape, kv_pool.dtype),
            pltpu.VMEM((depth,) + kv_pool.shape[1:], kv_pool.dtype),
            pltpu.SemaphoreType.DMA((8,)),
        ],
        compiler_params=pltpu.CompilerParams(vmem_limit_bytes=60 * 1024 * 1024),
    )(mig_source, mig_lengths, block_lists, kv_pool)


def relay_kernel(source_ref, target_ref, held_ref, terms_ref, out_ref, source_of):
    depth = held_ref.shape[0]
    rows = held_ref.shape[1]
    group = 8

    terms = terms_ref[...]
    for r in range(depth):
        source_of[target_ref[r]] = source_ref[r]
    for first in range(0, depth, group):
        pieces = []
        for t in range(first, first + group):
            pieces.append(held_ref[source_of[t]])
            pieces.append(terms[t * SLOTS : (t + 1) * SLOTS])
        size = (rows + SLOTS) * group
        whole = jnp.concatenate(pieces, axis=0)
        out_ref[pl.ds(first * (rows + SLOTS), size)] = whole.astype(out_ref.dtype)


def order_by_target(mig_source, mig_target, held, terms):
    smem = pl.BlockSpec(memory_space=pltpu.SMEM)
    vmem = pl.BlockSpec(memory_space=pltpu.VMEM)
    return pl.pallas_call(
        relay_kernel,
        in_specs=[smem, smem, vmem, vmem],
        out_specs=vmem,
        out_shape=jax.ShapeDtypeStruct(
            (held.shape[0] * (held.shape[1] + SLOTS), held.shape[2]), held.dtype
        ),
        scratch_shapes=[pltpu.SMEM(mig_target.shape, jnp.int32)],
        compiler_params=pltpu.CompilerParams(vmem_limit_bytes=16 * 1024 * 1024),
    )(mig_source, mig_target, held, terms)


def split_kernel(landed_ref, arrived_hbm, sums_ref, stage, sems):
    depth, rows = stage.shape[:2]
    group = 8
    total = jnp.zeros(sums_ref.shape, jnp.float32)
    writes = []
    for first in range(0, depth, group):
        size = (rows + SLOTS) * group
        whole = landed_ref[pl.ds(first * (rows + SLOTS), size)]
        for j in range(group):
            base = j * (rows + SLOTS)
            stage[first + j] = whole[base : base + rows].astype(stage.dtype)
            total = total + whole[base + rows : base + rows + SLOTS].astype(jnp.float32)
        part = pl.ds(first, group)
        writes.append(pltpu.make_async_copy(stage.at[part], arrived_hbm.at[part], sems.at[first // group]))
        writes[-1].start()
    sums_ref[...] = total
    for write in writes:
        write.wait()


def split_landed(landed, depth):
    rows = landed.shape[0] // depth - SLOTS
    width = landed.shape[1]
    vmem = pl.BlockSpec(memory_space=pltpu.VMEM)
    return pl.pallas_call(
        split_kernel,
        in_specs=[vmem],
        out_specs=[pl.BlockSpec(memory_space=pl.ANY), vmem],
        out_shape=[
            jax.ShapeDtypeStruct((depth, rows, width), landed.dtype),
            jax.ShapeDtypeStruct((SLOTS, width), jnp.float32),
        ],
        scratch_shapes=[
            pltpu.VMEM((depth, rows, width), landed.dtype),
            pltpu.SemaphoreType.DMA((depth // 8,)),
        ],
        compiler_params=pltpu.CompilerParams(vmem_limit_bytes=16 * 1024 * 1024),
    )(landed)


def local(
    queries,
    cache_keys,
    cache_values,
    new_keys,
    new_values,
    kv_pool,
    mig_lengths,
    mig_source,
    mig_target,
    block_lists,
    owner_map,
    check_key,
):
    attention = decode_attention(queries, cache_keys, cache_values, new_keys, new_values)
    members = lax.axis_size("inst")
    heads = lax.axis_size("tp")
    own_request, blocks = take_blocks(mig_source, mig_lengths, block_lists, kv_pool)
    own_request = own_request[0]
    width = blocks.shape[-1]
    sectioned = lax.all_to_all(blocks, "inst", split_axis=0, concat_axis=0, tiled=True)

    projected = jnp.einsum("blktd,lkde->blkte", blocks, check_key, preferred_element_type=jnp.float32)
    digest = jnp.sum(jnp.tanh(projected), axis=(1, 2, 3)) / 16.0
    owners = owner_map[own_request]
    table_rows = SLOTS * members
    one_hot = (owners[None, :] == jnp.arange(table_rows)[:, None]).astype(jnp.float32)
    table = jnp.dot(one_hot, digest, precision=lax.Precision.HIGHEST, preferred_element_type=jnp.float32)
    reach = 1
    while reach < heads:
        table = table + lax.ppermute(table, "tp", [(i, i ^ reach) for i in range(heads)])
        reach *= 2
    terms = table.astype(jnp.bfloat16)

    terms, attention = lax.optimization_barrier((terms, attention))

    onward = order_by_target(mig_source, mig_target, sectioned.reshape(members, -1, width), terms)
    landed = lax.all_to_all(
        onward.reshape(members, -1, SLOTS, width), "inst", split_axis=0, concat_axis=0, tiled=True
    )
    arrived, checksums = split_landed(landed.reshape(onward.shape), members)
    arrived = arrived.reshape(blocks.shape)
    return (attention, arrived, checksums)


def solution(mesh):
    placed = (
        P(None, None, "inst", "tp"),
        P(None, "inst", None, "tp"),
        P(None, "inst", None, "tp"),
        P(None, None, "inst", "tp"),
        P(None, None, "inst", "tp"),
        P("inst", None, None, None, "tp"),
        P(),
        P(),
        P(),
        P(),
        P(),
        P(None, None, "tp", None),
    )
    return jax.shard_map(
        local,
        mesh=mesh,
        in_specs=placed,
        out_specs=(P(None, None, "inst", "tp"), P("inst", None, None, None, "tp"), P("inst", None)),
        check_vma=False,
    )
```

```python
import math

import jax
import jax.numpy as jnp
from jax import lax
from jax.experimental import pallas as pl
from jax.experimental.pallas import tpu as pltpu
from jax.sharding import PartitionSpec as P

HD = 128
SLOTS = 2


def decode_attention(queries, cache_keys, cache_values, new_keys, new_values):
    layers, steps, requests, qwidth = queries.shape
    context = cache_keys.shape[2]
    kwidth = cache_keys.shape[3]
    heads_local = kwidth // HD
    grouping = qwidth // kwidth
    query = queries.reshape(layers, steps, requests, heads_local, grouping, HD)
    keyed = cache_keys.reshape(layers, requests, context, heads_local, HD)
    valued = cache_values.reshape(layers, requests, context, heads_local, HD)
    fresh_keys = new_keys.reshape(layers, steps, requests, heads_local, HD)
    fresh_values = new_values.reshape(layers, steps, requests, heads_local, HD)
    factor = 1.0 / math.sqrt(HD)
    old_scores = (
        jnp.einsum("lsrkgd,lrckd->lsrkgc", query, keyed, preferred_element_type=jnp.float32)
        * factor
    )
    new_scores = (
        jnp.einsum("lsrkgd,ltrkd->lsrkgt", query, fresh_keys, preferred_element_type=jnp.float32)
        * factor
    )
    order = jnp.arange(steps)
    visible = (order[None, :] <= order[:, None])[None, :, None, None, None, :]
    new_scores = jnp.where(visible, new_scores, -1e30)
    highest = jnp.maximum(
        jnp.max(old_scores, axis=-1, keepdims=True), jnp.max(new_scores, axis=-1, keepdims=True)
    )
    old_exp = jnp.exp(old_scores - highest)
    new_exp = jnp.where(visible, jnp.exp(new_scores - highest), 0.0)
    denominator = jnp.sum(old_exp, axis=-1, keepdims=True) + jnp.sum(
        new_exp, axis=-1, keepdims=True
    )
    old_weights = (old_exp / denominator).astype(jnp.bfloat16)
    new_weights = (new_exp / denominator).astype(jnp.bfloat16)
    mixed = jnp.einsum(
        "lsrkgc,lrckd->lsrkgd", old_weights, valued, preferred_element_type=jnp.float32
    )
    mixed = mixed + jnp.einsum(
        "lsrkgt,ltrkd->lsrkgd", new_weights, fresh_values, preferred_element_type=jnp.float32
    )
    return mixed.astype(jnp.bfloat16).reshape(layers, steps, requests, qwidth)


def take_kernel(
    source_hbm, length_hbm, list_hbm, pool_hbm, own_ref, stage, source, lengths, lists, pool, sems
):
    fetches = [
        pltpu.make_async_copy(*pair, sems.at[n])
        for n, pair in enumerate(
            [(source_hbm, source), (length_hbm, lengths), (list_hbm, lists), (pool_hbm, pool)]
        )
    ]
    for fetch in fetches:
        fetch.start()
    place = lax.axis_index("inst")
    depth, span = stage.shape[0], stage.shape[3]
    fetches[0].wait()
    own = jnp.int32(0)
    for i in range(source.shape[0]):
        own = jnp.where(source[i] == place, jnp.int32(i), own)
    own_ref[0] = own
    for fetch in fetches[1:]:
        fetch.wait()
    length = lengths[own]

    def clear(b, carry):
        block = stage[b]
        token = b * span + lax.broadcasted_iota(jnp.int32, block.shape, 2)
        stage[b] = jnp.where(token < length, block.astype(jnp.float32), 0.0).astype(block.dtype)
        return carry

    for b in range(depth):
        stage[b] = pool[lists[own, b]]
    lax.fori_loop(length // span, depth, clear, 0)


def take_blocks(mig_source, mig_lengths, block_lists, kv_pool):
    depth = block_lists.shape[1]
    return pl.pallas_call(
        take_kernel,
        in_specs=[pl.BlockSpec(memory_space=pltpu.HBM)] * 4,
        out_specs=[
            pl.BlockSpec(memory_space=pltpu.SMEM),
            pl.BlockSpec(memory_space=pltpu.VMEM),
        ],
        out_shape=[
            jax.ShapeDtypeStruct((1,), jnp.int32),
            jax.ShapeDtypeStruct((depth,) + kv_pool.shape[1:], kv_pool.dtype),
        ],
        scratch_shapes=[
            pltpu.SMEM(mig_source.shape, jnp.int32),
            pltpu.SMEM(mig_lengths.shape, jnp.int32),
            pltpu.SMEM(block_lists.shape, jnp.int32),
            pltpu.VMEM(kv_pool.shape, kv_pool.dtype),
            pltpu.SemaphoreType.DMA((4,)),
        ],
        compiler_params=pltpu.CompilerParams(vmem_limit_bytes=60 * 1024 * 1024),
    )(mig_source, mig_lengths, block_lists, kv_pool)


def relay_kernel(source_ref, target_ref, held_ref, terms_ref, out_ref, source_of):
    depth = held_ref.shape[0]
    rows = held_ref.shape[1]
    group = 8

    terms = terms_ref[...]
    for r in range(depth):
        source_of[target_ref[r]] = source_ref[r]
    for first in range(0, depth, group):
        pieces = []
        for t in range(first, first + group):
            pieces.append(held_ref[source_of[t]])
            pieces.append(terms[t * SLOTS : (t + 1) * SLOTS])
        size = (rows + SLOTS) * group
        whole = jnp.concatenate(pieces, axis=0)
        out_ref[pl.ds(first * (rows + SLOTS), size)] = whole.astype(out_ref.dtype)


def order_by_target(mig_source, mig_target, held, terms):
    smem = pl.BlockSpec(memory_space=pltpu.SMEM)
    vmem = pl.BlockSpec(memory_space=pltpu.VMEM)
    return pl.pallas_call(
        relay_kernel,
        in_specs=[smem, smem, vmem, vmem],
        out_specs=vmem,
        out_shape=jax.ShapeDtypeStruct(
            (held.shape[0] * (held.shape[1] + SLOTS), held.shape[2]), held.dtype
        ),
        scratch_shapes=[pltpu.SMEM(mig_target.shape, jnp.int32)],
        compiler_params=pltpu.CompilerParams(vmem_limit_bytes=16 * 1024 * 1024),
    )(mig_source, mig_target, held, terms)


def split_kernel(landed_ref, stage, sums_ref):
    depth, rows = stage.shape[:2]
    group = 8
    total = jnp.zeros(sums_ref.shape, jnp.float32)
    for first in range(0, depth, group):
        size = (rows + SLOTS) * group
        whole = landed_ref[pl.ds(first * (rows + SLOTS), size)]
        for j in range(group):
            base = j * (rows + SLOTS)
            stage[first + j] = whole[base : base + rows].astype(stage.dtype)
            total = total + whole[base + rows : base + rows + SLOTS].astype(jnp.float32)
    sums_ref[...] = total


def split_landed(landed, depth):
    rows = landed.shape[0] // depth - SLOTS
    width = landed.shape[1]
    vmem = pl.BlockSpec(memory_space=pltpu.VMEM)
    return pl.pallas_call(
        split_kernel,
        in_specs=[vmem],
        out_specs=[vmem, vmem],
        out_shape=[
            jax.ShapeDtypeStruct((depth, rows, width), landed.dtype),
            jax.ShapeDtypeStruct((SLOTS, width), jnp.float32),
        ],
        compiler_params=pltpu.CompilerParams(vmem_limit_bytes=16 * 1024 * 1024),
    )(landed)


def local(
    queries,
    cache_keys,
    cache_values,
    new_keys,
    new_values,
    kv_pool,
    mig_lengths,
    mig_source,
    mig_target,
    block_lists,
    owner_map,
    check_key,
):
    attention = decode_attention(queries, cache_keys, cache_values, new_keys, new_values)
    members = lax.axis_size("inst")
    heads = lax.axis_size("tp")
    own_request, blocks = take_blocks(mig_source, mig_lengths, block_lists, kv_pool)
    own_request = own_request[0]
    width = blocks.shape[-1]
    sectioned = lax.all_to_all(blocks, "inst", split_axis=0, concat_axis=0, tiled=True)

    projected = jnp.einsum("blktd,lkde->blkte", blocks, check_key, preferred_element_type=jnp.float32)
    digest = jnp.sum(jnp.tanh(projected), axis=(1, 2, 3)) / 16.0
    owners = owner_map[own_request]
    table_rows = SLOTS * members
    one_hot = (owners[None, :] == jnp.arange(table_rows)[:, None]).astype(jnp.float32)
    table = jnp.dot(one_hot, digest, precision=lax.Precision.HIGHEST, preferred_element_type=jnp.float32)
    reach = 1
    while reach < heads:
        table = table + lax.ppermute(table, "tp", [(i, i ^ reach) for i in range(heads)])
        reach *= 2
    terms = table.astype(jnp.bfloat16)

    terms, attention = lax.optimization_barrier((terms, attention))

    onward = order_by_target(mig_source, mig_target, sectioned.reshape(members, -1, width), terms)
    landed = lax.all_to_all(
        onward.reshape(members, -1, SLOTS, width), "inst", split_axis=0, concat_axis=0, tiled=True
    )
    arrived, checksums = split_landed(landed.reshape(onward.shape), members)
    arrived = arrived.reshape(blocks.shape)
    return (attention, arrived, checksums)


def solution(mesh):
    placed = (
        P(None, None, "inst", "tp"),
        P(None, "inst", None, "tp"),
        P(None, "inst", None, "tp"),
        P(None, None, "inst", "tp"),
        P(None, None, "inst", "tp"),
        P("inst", None, None, None, "tp"),
        P(),
        P(),
        P(),
        P(),
        P(),
        P(None, None, "tp", None),
    )
    return jax.shard_map(
        local,
        mesh=mesh,
        in_specs=placed,
        out_specs=(P(None, None, "inst", "tp"), P("inst", None, None, None, "tp"), P("inst", None)),
        check_vma=False,
    )
```

```python
import math

import jax
import jax.numpy as jnp
from jax import lax
from jax.experimental import pallas as pl
from jax.experimental.pallas import tpu as pltpu
from jax.sharding import PartitionSpec as P

HD = 128
SLOTS = 2


def decode_attention(queries, cache_keys, cache_values, new_keys, new_values):
    layers, steps, requests, qwidth = queries.shape
    context = cache_keys.shape[2]
    kwidth = cache_keys.shape[3]
    heads_local = kwidth // HD
    grouping = qwidth // kwidth
    query = queries.reshape(layers, steps, requests, heads_local, grouping, HD)
    keyed = cache_keys.reshape(layers, requests, context, heads_local, HD)
    valued = cache_values.reshape(layers, requests, context, heads_local, HD)
    fresh_keys = new_keys.reshape(layers, steps, requests, heads_local, HD)
    fresh_values = new_values.reshape(layers, steps, requests, heads_local, HD)
    factor = 1.0 / math.sqrt(HD)
    old_scores = (
        jnp.einsum("lsrkgd,lrckd->lsrkgc", query, keyed, preferred_element_type=jnp.float32)
        * factor
    )
    new_scores = (
        jnp.einsum("lsrkgd,ltrkd->lsrkgt", query, fresh_keys, preferred_element_type=jnp.float32)
        * factor
    )
    order = jnp.arange(steps)
    visible = (order[None, :] <= order[:, None])[None, :, None, None, None, :]
    new_scores = jnp.where(visible, new_scores, -1e30)
    highest = jnp.maximum(
        jnp.max(old_scores, axis=-1, keepdims=True), jnp.max(new_scores, axis=-1, keepdims=True)
    )
    old_exp = jnp.exp(old_scores - highest)
    new_exp = jnp.where(visible, jnp.exp(new_scores - highest), 0.0)
    denominator = jnp.sum(old_exp, axis=-1, keepdims=True) + jnp.sum(
        new_exp, axis=-1, keepdims=True
    )
    old_weights = (old_exp / denominator).astype(jnp.bfloat16)
    new_weights = (new_exp / denominator).astype(jnp.bfloat16)
    mixed = jnp.einsum(
        "lsrkgc,lrckd->lsrkgd", old_weights, valued, preferred_element_type=jnp.float32
    )
    mixed = mixed + jnp.einsum(
        "lsrkgt,ltrkd->lsrkgd", new_weights, fresh_values, preferred_element_type=jnp.float32
    )
    return mixed.astype(jnp.bfloat16).reshape(layers, steps, requests, qwidth)


def take_kernel(
    source_hbm, length_hbm, list_hbm, pool_hbm, own_ref, stage, source, lengths, lists, pool, sems
):
    fetches = [
        pltpu.make_async_copy(*pair, sems.at[n])
        for n, pair in enumerate(
            [(source_hbm, source), (length_hbm, lengths), (list_hbm, lists), (pool_hbm, pool)]
        )
    ]
    for fetch in fetches:
        fetch.start()
    place = lax.axis_index("inst")
    depth, span = stage.shape[0], stage.shape[3]
    fetches[0].wait()
    own = jnp.int32(0)
    for i in range(source.shape[0]):
        own = jnp.where(source[i] == place, jnp.int32(i), own)
    own_ref[0] = own
    for fetch in fetches[1:]:
        fetch.wait()
    length = lengths[own]

    def clear(b, carry):
        block = stage[b]
        token = b * span + lax.broadcasted_iota(jnp.int32, block.shape, 2)
        stage[b] = jnp.where(token < length, block.astype(jnp.float32), 0.0).astype(block.dtype)
        return carry

    for b in range(depth):
        stage[b] = pool[lists[own, b]]
    lax.fori_loop(length // span, depth, clear, 0)


def take_blocks(mig_source, mig_lengths, block_lists, kv_pool):
    depth = block_lists.shape[1]
    return pl.pallas_call(
        take_kernel,
        in_specs=[pl.BlockSpec(memory_space=pltpu.HBM)] * 4,
        out_specs=[
            pl.BlockSpec(memory_space=pltpu.SMEM),
            pl.BlockSpec(memory_space=pltpu.VMEM),
        ],
        out_shape=[
            jax.ShapeDtypeStruct((1,), jnp.int32),
            jax.ShapeDtypeStruct((depth,) + kv_pool.shape[1:], kv_pool.dtype),
        ],
        scratch_shapes=[
            pltpu.SMEM(mig_source.shape, jnp.int32),
            pltpu.SMEM(mig_lengths.shape, jnp.int32),
            pltpu.SMEM(block_lists.shape, jnp.int32),
            pltpu.VMEM(kv_pool.shape, kv_pool.dtype),
            pltpu.SemaphoreType.DMA((4,)),
        ],
        compiler_params=pltpu.CompilerParams(vmem_limit_bytes=60 * 1024 * 1024),
    )(mig_source, mig_lengths, block_lists, kv_pool)


def relay_kernel(source_of, held_ref, terms_ref, out_ref):
    depth = held_ref.shape[0]
    rows = held_ref.shape[1]
    group = 8

    terms = terms_ref[...]
    for first in range(0, depth, group):
        pieces = []
        for t in range(first, first + group):
            pieces.append(held_ref[source_of[t]])
            pieces.append(terms[t * SLOTS : (t + 1) * SLOTS])
        size = (rows + SLOTS) * group
        whole = jnp.concatenate(pieces, axis=0)
        out_ref[pl.ds(first * (rows + SLOTS), size)] = whole.astype(out_ref.dtype)


def order_by_target(source_of, held, terms):
    smem = pl.BlockSpec(memory_space=pltpu.SMEM)
    vmem = pl.BlockSpec(memory_space=pltpu.VMEM)
    return pl.pallas_call(
        relay_kernel,
        in_specs=[smem, vmem, vmem],
        out_specs=vmem,
        out_shape=jax.ShapeDtypeStruct(
            (held.shape[0] * (held.shape[1] + SLOTS), held.shape[2]), held.dtype
        ),
        compiler_params=pltpu.CompilerParams(vmem_limit_bytes=16 * 1024 * 1024),
    )(source_of, held, terms)


def split_kernel(landed_ref, stage, sums_ref):
    depth, rows = stage.shape[:2]
    group = 8
    total = jnp.zeros(sums_ref.shape, jnp.float32)
    for first in range(0, depth, group):
        size = (rows + SLOTS) * group
        whole = landed_ref[pl.ds(first * (rows + SLOTS), size)]
        for j in range(group):
            base = j * (rows + SLOTS)
            stage[first + j] = whole[base : base + rows].astype(stage.dtype)
            total = total + whole[base + rows : base + rows + SLOTS].astype(jnp.float32)
    sums_ref[...] = total


def split_landed(landed, depth):
    rows = landed.shape[0] // depth - SLOTS
    width = landed.shape[1]
    vmem = pl.BlockSpec(memory_space=pltpu.VMEM)
    return pl.pallas_call(
        split_kernel,
        in_specs=[vmem],
        out_specs=[vmem, vmem],
        out_shape=[
            jax.ShapeDtypeStruct((depth, rows, width), landed.dtype),
            jax.ShapeDtypeStruct((SLOTS, width), jnp.float32),
        ],
        compiler_params=pltpu.CompilerParams(vmem_limit_bytes=16 * 1024 * 1024),
    )(landed)


def local(
    queries,
    cache_keys,
    cache_values,
    new_keys,
    new_values,
    kv_pool,
    mig_lengths,
    mig_source,
    mig_target,
    block_lists,
    owner_map,
    check_key,
):
    attention = decode_attention(queries, cache_keys, cache_values, new_keys, new_values)
    members = lax.axis_size("inst")
    heads = lax.axis_size("tp")
    own_request, blocks = take_blocks(mig_source, mig_lengths, block_lists, kv_pool)
    own_request = own_request[0]
    width = blocks.shape[-1]
    sectioned = lax.all_to_all(blocks, "inst", split_axis=0, concat_axis=0, tiled=True)

    projected = jnp.einsum("blktd,lkde->blkte", blocks, check_key, preferred_element_type=jnp.float32)
    digest = jnp.sum(jnp.tanh(projected), axis=(1, 2, 3)) / 16.0
    owners = owner_map[own_request]
    table_rows = SLOTS * members
    one_hot = (owners[None, :] == jnp.arange(table_rows)[:, None]).astype(jnp.float32)
    table = jnp.dot(one_hot, digest, precision=lax.Precision.HIGHEST, preferred_element_type=jnp.float32)
    reach = 1
    while reach < heads:
        table = table + lax.ppermute(table, "tp", [(i, i ^ reach) for i in range(heads)])
        reach *= 2
    terms = table.astype(jnp.bfloat16)

    source_of = jnp.sum(
        jnp.where(mig_target[None, :] == jnp.arange(members)[:, None], mig_source[None, :], 0), axis=1
    )
    terms, attention, source_of = lax.optimization_barrier((terms, attention, source_of))

    onward = order_by_target(source_of, sectioned.reshape(members, -1, width), terms)
    landed = lax.all_to_all(
        onward.reshape(members, -1, SLOTS, width), "inst", split_axis=0, concat_axis=0, tiled=True
    )
    arrived, checksums = split_landed(landed.reshape(onward.shape), members)
    arrived = arrived.reshape(blocks.shape)
    return (attention, arrived, checksums)


def solution(mesh):
    placed = (
        P(None, None, "inst", "tp"),
        P(None, "inst", None, "tp"),
        P(None, "inst", None, "tp"),
        P(None, None, "inst", "tp"),
        P(None, None, "inst", "tp"),
        P("inst", None, None, None, "tp"),
        P(),
        P(),
        P(),
        P(),
        P(),
        P(None, None, "tp", None),
    )
    return jax.shard_map(
        local,
        mesh=mesh,
        in_specs=placed,
        out_specs=(P(None, None, "inst", "tp"), P("inst", None, None, None, "tp"), P("inst", None)),
        check_vma=False,
    )
```
